512 devices in a mesh: dp: 32 (over y, z_hi, core), shard: 16 (over x, z_lo).
Axes of the slice: x: 4, y: 4, z: 16 (z_hi: 4, z_lo: 4; z = z_hi * 4 + z_lo), core: 2. Of those that a mesh axis runs over, the one named last changes fastest.
Arguments:
- ffn_input: bfloat16 [16384, 8192], P('dp', 'shard'), may hold values from -6 to 6
- up_cotangent: bfloat16 [16384, 28672], P('dp', 'shard'), may hold values from -0.059814453 to 0.059814453
- projector: bfloat16 [8192, 512], P('shard'), may hold values from -0.0625 to 0.0625
- first_moment: float32 [512, 28672], P('dp', 'shard'), may hold values from -0.6 to 0.6
- second_moment: float32 [512, 28672], P('dp', 'shard'), may hold values from 0.0001 to 0.01
Outputs:
- expanded_step: bfloat16 [8192, 28672], P('dp', 'shard')
- first_next: float32 [512, 28672], P('dp', 'shard')
- second_next: float32 [512, 28672], P('dp', 'shard')
The draws below stay inside these ranges and needn't reach their ends.
All inputs are finite; a program needn't handle non-finite values.
Results may differ from the reference program's by a relative error of at most 0.0061.
Values may be sent and summed in bfloat16 or wider, within the bound.
No kernel may reach another device: no remote copies, remote signals or barrier semaphores. Data moves between devices by JAX's collectives and lax.ppermute only.
A program may use at most 64 MiB of HBM per device.

```python
import math
import jax
import jax.numpy as jnp

D = 8192
FF = 28672
RANK = 512
STEP = 10
TOKENS = 16384


def block_levels(rng, dims, shards, smallest, largest):
    level = 1.0
    for position, shards_of in shards:
        draws = jax.random.uniform(jax.random.fold_in(jax.random.fold_in(rng, 6), position), (shards_of,), jnp.float32, smallest / len(shards), largest / len(shards))
        level = level * jnp.repeat(jnp.exp(draws), dims[position] // shards_of).reshape((-1,) + (1,) * (len(dims) - 1 - position))
    return level


def normal_values(stream_key, extent, spread, most, shards=(), kind=jnp.bfloat16):
    result = spread * jax.random.normal(stream_key, extent, jnp.float32)
    if shards:
        result = result * block_levels(stream_key, extent, shards, -0.22, 0.18)
    return jnp.clip(result, -most, most).astype(kind)


def setup_inputs(seed: int = 0) -> dict:
    keys = jax.random.split(jax.random.key(seed), 6)
    ffn_input = normal_values(keys[0], (TOKENS, D), 1.0, 6.0, ((0, 32), (1, 16)))
    up_cotangent = normal_values(keys[1], (TOKENS, FF), 0.01, 0.059814453, ((0, 32), (1, 16)))
    projector = normal_values(keys[2], (D, RANK), D ** -0.5, 0.0625, ((0, 16),))
    first_moment = normal_values(keys[3], (RANK, FF), 0.1, 0.6, ((0, 32), (1, 16)), jnp.float32)
    second_moment = jnp.clip(jnp.exp(math.log(0.01) - 4.6051702 * jax.random.uniform(keys[4], (RANK, FF), jnp.float32) ** block_levels(keys[4], (RANK, FF), ((0, 32), (1, 16)), -0.2, 0.2)), 0.0001, 0.01)
    return dict(ffn_input=ffn_input, up_cotangent=up_cotangent, projector=projector, first_moment=first_moment, second_moment=second_moment)


beta_first = 0.9
beta_second = 0.999
epsilon = 1e-08

def reference(ffn_input, up_cotangent, projector, first_moment, second_moment):
    projected = jnp.dot(ffn_input, projector, preferred_element_type=jnp.float32).astype(jnp.bfloat16)
    low_grad = jnp.dot(projected.T, up_cotangent, preferred_element_type=jnp.float32)
    first_next = beta_first * first_moment + (1.0 - beta_first) * low_grad
    second_next = beta_second * second_moment + (1.0 - beta_second) * low_grad * low_grad
    first_hat = first_next / (1.0 - beta_first ** STEP)
    second_hat = second_next / (1.0 - beta_second ** STEP)
    normalized = (first_hat / (jnp.sqrt(second_hat) + epsilon)).astype(jnp.bfloat16)
    expanded_step = jnp.dot(projector, normalized, preferred_element_type=jnp.float32).astype(jnp.bfloat16)
    return (expanded_step, first_next, second_next)
```

```python
import jax
import jax.numpy as jnp
import numpy as np
from jax import lax
from jax.sharding import Mesh, PartitionSpec as P

STEP = 10

beta_first = 0.9
beta_second = 0.999
epsilon = 1e-08

AXES = ("y", "zh", "core", "x", "zl")
DP = ("y", "zh", "core")
SHARD = ("x", "zl")
bf16 = jnp.bfloat16
f32 = jnp.float32


def dot(a, b):
    return jnp.dot(a, b, preferred_element_type=f32)


def swap_cores(a):
    return lax.ppermute(a, "core", [(0, 1), (1, 0)])


def pick_half(ranks, core):
    rank = lax.broadcasted_iota(jnp.int32, (ranks, ranks // 2), 0)
    at = lax.broadcasted_iota(jnp.int32, (ranks, ranks // 2), 1)
    rows = ranks // 32
    return (rank == (at // rows) * (2 * rows) + core * rows + at % rows).astype(bf16)


def exchange(a, axes, n):
    return lax.all_to_all(a.reshape(n, a.shape[0] // n, a.shape[1]), axes, 0, 0)


def spread(a, axes, n):
    got = lax.all_to_all(jnp.broadcast_to(a, (n, *a.shape)), axes, 0, 0)
    return got.reshape(n * a.shape[0], a.shape[1])


def transposed_pairs():
    ids = np.arange(512).reshape(4, 4, 2, 4, 4)
    return [(int(s), int(d)) for s, d in zip(ids.transpose(3, 4, 2, 0, 1).ravel(), ids.ravel())]


def adam_update(low_grad, first_moment, second_moment):
    first_next = beta_first * first_moment + (1.0 - beta_first) * low_grad
    second_next = beta_second * second_moment + (1.0 - beta_second) * low_grad * low_grad
    first_hat = first_next / (1.0 - beta_first**STEP)
    second_hat = second_next / (1.0 - beta_second**STEP)
    normalized = (first_hat / (jnp.sqrt(second_hat) + epsilon)).astype(bf16)
    return (first_next, second_next, normalized)


def on_device(ffn_input, up_cotangent, projector, first_moment, second_moment):
    tokens, ranks = ffn_input.shape[0], projector.shape[1]
    core = lax.axis_index("core")
    other_input = swap_cores(ffn_input)
    own_half = pick_half(ranks, core)
    half_basis = dot(projector, own_half).astype(bf16)
    local = jnp.concatenate([dot(ffn_input, half_basis), dot(other_input, half_basis)], 0)
    other_cotangent = swap_cores(up_cotangent)
    basis_rows = lax.ppermute(
        lax.dynamic_slice_in_dim(projector, core * 256, 256, 0), AXES, transposed_pairs()
    )
    parts = exchange(local.astype(bf16), SHARD, 16)
    mine = jnp.sum(parts.astype(f32), 0).astype(bf16)
    mine, basis_rows = lax.optimization_barrier((mine, basis_rows))
    projected = spread(mine, SHARD, 16)

    grad = dot(projected[:tokens].T, up_cotangent) + dot(projected[tokens:].T, other_cotangent)
    grad = jnp.sum(exchange(grad.astype(bf16), "y", 4).astype(f32), 0)
    low_grad = jnp.sum(exchange(grad.astype(bf16), "zh", 4).astype(f32), 0)
    first_next, second_next, normalized = adam_update(low_grad, first_moment, second_moment)

    own_step = spread(spread(normalized, "zh", 4), "y", 4)
    other_step = swap_cores(own_step)
    own_rows = dot(basis_rows, own_half).astype(bf16)
    other_rows = dot(basis_rows, pick_half(ranks, 1 - core)).astype(bf16)
    expanded_step = (dot(own_rows, own_step) + dot(other_rows, other_step)).astype(bf16)
    return (expanded_step, first_next, second_next)


def solution(mesh):
    split = Mesh(mesh.devices.reshape(4, 4, 2, 4, 4), AXES)
    in_specs = (
        P(DP, SHARD),
        P(DP, SHARD),
        P(SHARD, None),
        P(DP, SHARD),
        P(DP, SHARD),
    )
    out_specs = (P(DP, SHARD), P(DP, SHARD), P(DP, SHARD))
    return jax.shard_map(
        on_device, mesh=split, in_specs=in_specs, out_specs=out_specs, check_vma=False
    )
```

```python
import jax
import jax.numpy as jnp
import numpy as np
from jax import lax
from jax.sharding import Mesh, PartitionSpec as P

STEP = 10

beta_first = 0.9
beta_second = 0.999
epsilon = 1e-08

AXES = ("y", "zh", "core", "x", "zl")
DP = ("y", "zh", "core")
SHARD = ("x", "zl")
bf16 = jnp.bfloat16
f32 = jnp.float32

NEAR = ((0, 3, 1, 2), (2, 0, 3, 1), (3, 0, 1, 2), (2, 3, 0, 1))


def dot(a, b):
    return jnp.dot(a, b, preferred_element_type=f32)


def dot_rows(a, b):
    return lax.dot_general(a, b, (((0,), (0,)), ((), ())), preferred_element_type=f32)


def swap_cores(a):
    return lax.ppermute(a, "core", [(0, 1), (1, 0)])


def pick_half(ranks, core):
    rank = lax.broadcasted_iota(jnp.int32, (ranks, ranks // 2), 0)
    at = lax.broadcasted_iota(jnp.int32, (ranks, ranks // 2), 1)
    rows = ranks // 32
    return (rank == (at // rows) * (2 * rows) + core * rows + at % rows).astype(bf16)


def pick_all(ranks):
    return jnp.concatenate([pick_half(ranks, 0), pick_half(ranks, 1)], 1)


def exchange(a, axes, n):
    return lax.all_to_all(a.reshape(n, a.shape[0] // n, a.shape[1]), axes, 0, 0)


def add_up(parts):
    total = parts[0].astype(f32)
    for i in range(1, parts.shape[0]):
        total = total + parts[i].astype(f32)
    return total


def spread(a, axes, n):
    got = lax.all_to_all(jnp.broadcast_to(a, (n, *a.shape)), axes, 0, 0)
    return got.reshape(n * a.shape[0], a.shape[1])


STEPS = [('x', 2), ('z', 2), ('z', 1), ('x', 1)]


def hand_on(a, step):
    ids = np.arange(512).reshape(4, 4, 2, 4, 4)
    has = [(0, 0)]
    for axis, bit in STEPS[: STEPS.index(step)]:
        has += [(dx ^ bit, dz) if axis == "x" else (dx, dz ^ bit) for dx, dz in has]
    pairs = []
    for y, zh, c in np.ndindex(4, 4, 2):
        for dx, dz in has:
            to = (dx ^ step[1], dz) if step[0] == "x" else (dx, dz ^ step[1])
            pairs.append(
                (int(ids[y, zh, c, y ^ dx, zh ^ dz]), int(ids[y, zh, c, y ^ to[0], zh ^ to[1]]))
            )
    return lax.ppermute(a, AXES, pairs)


def adam_update(low_grad, first_moment, second_moment):
    first_next = beta_first * first_moment + (1.0 - beta_first) * low_grad
    second_next = beta_second * second_moment + (1.0 - beta_second) * low_grad * low_grad
    first_hat = first_next / (1.0 - beta_first**STEP)
    second_hat = second_next / (1.0 - beta_second**STEP)
    normalized = (first_hat / (jnp.sqrt(second_hat) + epsilon)).astype(bf16)
    return (first_next, second_next, normalized)


def on_device(ffn_input, up_cotangent, projector, first_moment, second_moment):
    tokens, ranks = ffn_input.shape[0], projector.shape[1]
    half = ranks // 2
    core = lax.axis_index("core")
    other_cotangent = swap_cores(up_cotangent)
    ordered = lax.optimization_barrier(dot(projector, pick_all(ranks)).astype(bf16))
    rows = ordered.shape[0] // 2
    has_rows = (lax.axis_index("x") == lax.axis_index("y")) & (
        lax.axis_index("zl") == lax.axis_index("zh")
    )
    basis = lax.dynamic_slice_in_dim(ordered, core * rows, rows, 0)
    basis = jnp.where(has_rows, basis, 0)
    local = dot(ffn_input, ordered).astype(bf16)
    local, basis = lax.optimization_barrier((local, basis))
    came = hand_on(basis, ('x', 2))
    parts, came = lax.optimization_barrier((exchange(local, SHARD, 16), came))
    basis = basis + came
    mine = add_up(parts).astype(bf16)
    halves = jnp.stack([mine[:, :half], mine[:, half:]], 0)
    halves = jnp.broadcast_to(halves[:, None], (2, 16, *halves.shape[1:]))
    halves = halves.reshape(32, *halves.shape[2:])
    got = lax.all_to_all(halves, ("core", *SHARD), 0, 0)
    projected = got.reshape(2, tokens, half)
    own = lax.dynamic_index_in_dim(projected, core, 0, False)
    other = lax.dynamic_index_in_dim(projected, 1 - core, 0, False)
    grad = dot_rows(own, up_cotangent) + dot_rows(other, other_cotangent)
    grad = grad.astype(bf16)
    grad, basis = lax.optimization_barrier((grad, basis))
    basis = basis + hand_on(basis, ('z', 2))
    came = hand_on(basis, ('z', 1))
    grad, came = lax.optimization_barrier((exchange(grad, "y", 4), came))
    basis = basis + came
    grad = add_up(grad).astype(bf16)
    grad, basis = lax.optimization_barrier((grad, basis))
    came = hand_on(basis, ('x', 1))
    grad, came = lax.optimization_barrier((exchange(grad, "zh", 4), came))
    basis = basis + came
    low_grad = add_up(grad)
    first_next, second_next, normalized = adam_update(low_grad, first_moment, second_moment)
    quarter_step = spread(normalized, "zh", 4)
    own_step = spread(quarter_step, "y", 4)
    low_rows, high_rows = basis[:, :half], basis[:, half:]
    other_step = swap_cores(own_step)
    own_rows = jnp.where(core == 0, low_rows, high_rows)
    other_rows = jnp.where(core == 0, high_rows, low_rows)
    expanded_step = (dot(own_rows, own_step) + dot(other_rows, other_step)).astype(bf16)
    return (expanded_step, first_next, second_next)


def solution(mesh):
    split = Mesh(mesh.devices.reshape(4, 4, 2, 4, 4), AXES)
    in_specs = (
        P(DP, SHARD),
        P(DP, SHARD),
        P(SHARD, None),
        P(DP, SHARD),
        P(DP, SHARD),
    )
    out_specs = (P(DP, SHARD), P(DP, SHARD), P(DP, SHARD))
    return jax.shard_map(
        on_device, mesh=split, in_specs=in_specs, out_specs=out_specs, check_vma=False
    )
```

```python
import jax
import jax.numpy as jnp
import numpy as np
from jax import lax
from jax.experimental import pallas as pl
from jax.experimental.layout import Layout, with_layout_constraint
from jax.experimental.pallas import tpu as pltpu
from jax.sharding import Mesh, PartitionSpec as P

STEP = 10

beta_first = 0.9
beta_second = 0.999
epsilon = 1e-08

AXES = ("y", "zh", "core", "x", "zl")
DP = ("y", "zh", "core")
SHARD = ("x", "zl")
bf16 = jnp.bfloat16
f32 = jnp.float32

NEAR = ((0, 3, 1, 2), (2, 0, 3, 1), (3, 0, 1, 2), (2, 3, 0, 1))


def dot(a, b):
    return jnp.dot(a, b, preferred_element_type=f32)


def dot_rows(a, b):
    return lax.dot_general(a, b, (((0,), (0,)), ((), ())), preferred_element_type=f32)


def swap_cores(a):
    return lax.ppermute(a, "core", [(0, 1), (1, 0)])


def pick_half(ranks, core):
    rank = lax.broadcasted_iota(jnp.int32, (ranks, ranks // 2), 0)
    at = lax.broadcasted_iota(jnp.int32, (ranks, ranks // 2), 1)
    rows = ranks // 32
    return (rank == (at // rows) * (2 * rows) + core * rows + at % rows).astype(bf16)


def pick_all(ranks):
    return jnp.concatenate([pick_half(ranks, 0), pick_half(ranks, 1)], 1)


def exchange(a, axes, n):
    return lax.all_to_all(a.reshape(n, a.shape[0] // n, a.shape[1]), axes, 0, 0)


def add_up(parts):
    total = parts[0].astype(f32)
    for i in range(1, parts.shape[0]):
        total = total + parts[i].astype(f32)
    return total


def spread(a, axes, n):
    got = lax.all_to_all(jnp.broadcast_to(a, (n, *a.shape)), axes, 0, 0)
    return got.reshape(n * a.shape[0], a.shape[1])


STEPS = [('x', 2), ('z', 2), ('z', 1), ('x', 1)]


def hand_on(a, step):
    ids = np.arange(512).reshape(4, 4, 2, 4, 4)
    has = [(0, 0)]
    for axis, bit in STEPS[: STEPS.index(step)]:
        has += [(dx ^ bit, dz) if axis == "x" else (dx, dz ^ bit) for dx, dz in has]
    pairs = []
    for y, zh, c in np.ndindex(4, 4, 2):
        for dx, dz in has:
            to = (dx ^ step[1], dz) if step[0] == "x" else (dx, dz ^ step[1])
            pairs.append(
                (int(ids[y, zh, c, y ^ dx, zh ^ dz]), int(ids[y, zh, c, y ^ to[0], zh ^ to[1]]))
            )
    return lax.ppermute(a, AXES, pairs)


def adam_update(low_grad, first_moment, second_moment):
    first_next = beta_first * first_moment + (1.0 - beta_first) * low_grad
    second_next = beta_second * second_moment + (1.0 - beta_second) * low_grad * low_grad
    first_hat = first_next / (1.0 - beta_first**STEP)
    second_hat = second_next / (1.0 - beta_second**STEP)
    normalized = (first_hat / (jnp.sqrt(second_hat) + epsilon)).astype(bf16)
    return (first_next, second_next, normalized)


def low_grad_kernel(core_ref, projected, own_cotangent, other_cotangent, out):
    core = core_ref[0]
    own, other = projected[core], projected[1 - core]
    width = 256
    for at in range(0, out.shape[1], width):
        cols = pl.ds(at, width)
        total = dot_rows(own, own_cotangent[:, cols]) + dot_rows(other, other_cotangent[:, cols])
        out[:, cols] = total.astype(bf16)


def low_grad_part(core, projected, own_cotangent, other_cotangent):
    vmem = pl.BlockSpec(memory_space=pltpu.VMEM)
    flops = 2 * projected.size * own_cotangent.shape[1]
    return pl.pallas_call(
        low_grad_kernel,
        out_shape=jax.ShapeDtypeStruct((projected.shape[2], own_cotangent.shape[1]), bf16),
        in_specs=[pl.BlockSpec(memory_space=pltpu.SMEM), vmem, vmem, vmem],
        out_specs=vmem,
        compiler_params=pltpu.CompilerParams(vmem_limit_bytes=24 << 20),
        cost_estimate=pl.CostEstimate(flops=flops, bytes_accessed=5 << 20, transcendentals=0),
    )(core.reshape(1), projected, own_cotangent, other_cotangent)


def share_kernel(parts, out):
    total = parts[0].astype(f32)
    for i in range(1, parts.shape[0]):
        total = total + parts[i].astype(f32)
    mine = total.astype(bf16)
    half = out.shape[3]
    for c in range(2):
        for i in range(out.shape[1]):
            out[c, i] = mine[:, c * half : (c + 1) * half]


def share(parts):
    n, rows, ranks = parts.shape
    vmem = pl.BlockSpec(memory_space=pltpu.VMEM)
    return pl.pallas_call(
        share_kernel,
        out_shape=jax.ShapeDtypeStruct((2, n, rows, ranks // 2), bf16),
        in_specs=[vmem],
        out_specs=vmem,
        compiler_params=pltpu.CompilerParams(vmem_limit_bytes=8 << 20),
        cost_estimate=pl.CostEstimate(flops=parts.size, bytes_accessed=1 << 20, transcendentals=0),
    )(parts)


def on_device(ffn_input, up_cotangent, projector, first_moment, second_moment):
    tokens, ranks = ffn_input.shape[0], projector.shape[1]
    half = ranks // 2
    core = lax.axis_index("core")
    other_cotangent = swap_cores(up_cotangent)
    ordered = lax.optimization_barrier(dot(projector, pick_all(ranks)).astype(bf16))
    rows = ordered.shape[0] // 2
    has_rows = (lax.axis_index("x") == lax.axis_index("y")) & (
        lax.axis_index("zl") == lax.axis_index("zh")
    )
    basis = lax.dynamic_slice_in_dim(ordered, core * rows, rows, 0)
    basis = jnp.where(has_rows, basis, 0)
    local = dot(ffn_input, ordered).astype(bf16)
    local = with_layout_constraint(local, Layout((0, 1)))
    local, basis = lax.optimization_barrier((local, basis))
    came = hand_on(basis, ('x', 2))
    parts, came = lax.optimization_barrier((exchange(local, SHARD, 16), came))
    basis = basis + came
    halves = share(parts)
    halves = halves.reshape(32, *halves.shape[2:])
    got = lax.all_to_all(halves, ("core", *SHARD), 0, 0)
    projected = got.reshape(2, tokens, half)
    grad = low_grad_part(core, projected, up_cotangent, other_cotangent)
    grad, basis = lax.optimization_barrier((grad, basis))
    basis = basis + hand_on(basis, ('z', 2))
    came = hand_on(basis, ('z', 1))
    grad, came = lax.optimization_barrier((exchange(grad, "y", 4), came))
    basis = basis + came
    grad = add_up(grad).astype(bf16)
    grad, basis = lax.optimization_barrier((grad, basis))
    came = hand_on(basis, ('x', 1))
    grad, came = lax.optimization_barrier((exchange(grad, "zh", 4), came))
    basis = basis + came
    low_grad = add_up(grad)
    first_next, second_next, normalized = adam_update(low_grad, first_moment, second_moment)
    quarter_step = spread(normalized, "zh", 4)
    own_step = spread(quarter_step, "y", 4)
    low_rows, high_rows = basis[:, :half], basis[:, half:]
    other_step = swap_cores(own_step)
    own_rows = jnp.where(core == 0, low_rows, high_rows)
    other_rows = jnp.where(core == 0, high_rows, low_rows)
    expanded_step = (dot(own_rows, own_step) + dot(other_rows, other_step)).astype(bf16)
    return (expanded_step, first_next, second_next)


def solution(mesh):
    split = Mesh(mesh.devices.reshape(4, 4, 2, 4, 4), AXES)
    in_specs = (
        P(DP, SHARD),
        P(DP, SHARD),
        P(SHARD, None),
        P(DP, SHARD),
        P(DP, SHARD),
    )
    out_specs = (P(DP, SHARD), P(DP, SHARD), P(DP, SHARD))
    return jax.shard_map(
        on_device, mesh=split, in_specs=in_specs, out_specs=out_specs, check_vma=False
    )
```
